1024 devices in a mesh: dp: 16 (over z, core), expert: 64 (over y, x).
Axes of the slice: x: 8, y: 8, z: 8, core: 2. Of those that a mesh axis runs over, the one named last changes fastest.
Arguments:
- tokens: bfloat16 [8192, 3584], P('expert', 'dp'), may hold values from -6 to 6
- cotangent: bfloat16 [8192, 3584], P('expert', 'dp'), may hold values from -6 to 6
- w_in: bfloat16 [64, 3584, 1024], P('expert', 'dp'), may hold values from -0.09375 to 0.09375
- w_out: bfloat16 [64, 1024, 3584], P('expert', None, 'dp'), may hold values from -0.1875 to 0.1875
- route_token: int32 [64, 64, 8], P('expert'), may hold values from 0 to 127
- route_count: int32 [64, 64], P('expert'), may hold values from 1 to 8, as said below
- copy_plan: int32 [64], replicated, may hold values from 0 to 1, as said below
- route_prob: float32 [64, 64, 8], P('expert'), may hold values from 0.05 to 1
Outputs:
- expert_out: bfloat16 [8192, 3584], P('expert', 'dp')
- token_grad: bfloat16 [8192, 3584], P('expert', 'dp')
- w_in_grad: bfloat16 [64, 3584, 1024], P('expert', 'dp')
- w_out_grad: bfloat16 [64, 1024, 3584], P('expert', None, 'dp')
The draws below stay inside these ranges and needn't reach their ends.
Inputs may be any that keep to these rules, and one draw needn't show every extreme that they name: `route_count`: every source routes exactly 8 rows to at least one expert, and each of the experts 0, 31, 32 and 63 receives exactly 8 rows from some source. copy_plan is 1 for experts 0, 31, 32 and 63.
All inputs are finite; a program needn't handle non-finite values.
Results may differ from the reference program's by a relative error of at most 0.0057.
Values may be sent and summed in bfloat16 or wider, within the bound.
A program may use at most 32 MiB of HBM per device.

```python
import math
import jax
import jax.numpy as jnp
from jax import lax

D = 3584
FF = 1024
TOK_DEV = 128
EXPERTS = 64
TOKENS = 8192
CAP = 8
CAP_HOME = 4
N_EXPERT = 64


def forced_experts():
    experts_index = jnp.arange(EXPERTS, dtype=jnp.int32)
    return (experts_index == 0) | (experts_index == EXPERTS // 2 - 1) | (experts_index == EXPERTS // 2) | (experts_index == EXPERTS - 1)


def draw_route_count(key, part):
    key = jax.random.fold_in(key, 5)
    draw_key, pick_key, source_key = jax.random.split(key, 3)
    counts = jax.random.randint(draw_key, (N_EXPERT, EXPERTS), 1, CAP + 1)
    fullest = jax.random.randint(pick_key, (N_EXPERT, 1), 0, EXPERTS)
    columns = jnp.arange(EXPERTS, dtype=jnp.int32)[None, :]
    counts = jnp.where(columns == fullest, CAP, counts)
    chosen_source = jax.random.randint(source_key, (1, EXPERTS), 0, N_EXPERT)
    rows_index = jnp.arange(N_EXPERT, dtype=jnp.int32)[:, None]
    full_here = forced_experts()[None, :] & (rows_index == chosen_source)
    return jnp.where(full_here, CAP, counts).astype(jnp.int32)


def draw_copy_plan(key, part):
    key = jax.random.fold_in(key, 7)
    plan = jax.random.randint(key, (EXPERTS,), 0, 2)
    return jnp.where(forced_experts(), 1, plan).astype(jnp.int32)


def touch_ends(entries, stream_key, least, top_value):
    dims = entries.shape
    place = [jax.random.randint(jax.random.fold_in(stream_key, axis), (), 0, dims[axis]) for axis in range(len(dims))]
    entries = entries.at[tuple(place)].set(least)
    longest = dims.index(max(dims))
    place[longest] = (place[longest] + 1) % dims[longest]
    return entries.at[tuple(place)].set(top_value)


def block_levels(stream_key, dims, cuts, smallest, top_value):
    def one(dim, shards_of):
        heights = jax.random.uniform(jax.random.fold_in(jax.random.fold_in(stream_key, 6), dim), (shards_of,), jnp.float32, smallest / len(cuts), top_value / len(cuts))
        return jnp.repeat(jnp.exp(heights), dims[dim] // shards_of).reshape((-1,) + (1,) * (len(dims) - dim - 1))

    gain = one(*cuts[0])
    for cut in cuts[1:]:
        gain = gain * one(*cut)
    return gain


def noise(key, shape, deviation, most, cuts=(), kind=jnp.bfloat16):
    values = deviation * jax.random.normal(key, shape, jnp.float32)
    if cuts:
        values = values * block_levels(key, shape, cuts, -0.22, 0.18)
    return jnp.clip(values, -most, most).astype(kind)


def setup_inputs(seed: int = 0) -> dict:
    splits = jax.random.split(jax.random.key(seed), 9)
    tokens = noise(splits[0], (TOKENS, D), 1.0, 6.0, ((0, 64), (1, 16)))
    cotangent = noise(splits[1], (TOKENS, D), 1.0, 6.0, ((0, 64), (1, 16)))
    w_in = noise(splits[2], (EXPERTS, D, FF), D ** -0.5, 0.09375, ((0, 64), (1, 16)))
    w_out = noise(splits[3], (EXPERTS, FF, D), FF ** -0.5, 0.1875, ((0, 64), (2, 16)))
    route_token = touch_ends(jax.random.randint(splits[4], (N_EXPERT, EXPERTS, CAP), 0, TOK_DEV), jax.random.fold_in(splits[4], 1), 0, TOK_DEV - 1).astype(jnp.int32)
    route_count = draw_route_count(jax.random.fold_in(splits[8], 71), 0)
    copy_plan = draw_copy_plan(jax.random.fold_in(splits[8], 71), 0)
    route_prob = jnp.clip(jnp.exp(math.log(1.0) - 2.9957323 * jax.random.uniform(splits[7], (N_EXPERT, EXPERTS, CAP), jnp.float32) ** block_levels(splits[7], (N_EXPERT, EXPERTS, CAP), ((0, 64),), -0.2, 0.2)), 0.05, 1.0)
    return dict(tokens=tokens, cotangent=cotangent, w_in=w_in, w_out=w_out, route_token=route_token, route_count=route_count, copy_plan=copy_plan, route_prob=route_prob)


def silu_slope(values):
    sigmoid_part = jax.nn.sigmoid(values)
    return sigmoid_part * (1.0 + values * (1.0 - sigmoid_part))


def reference(tokens, cotangent, w_in, w_out, route_token, route_count, copy_plan, route_prob):
    slot_index = jnp.arange(CAP, dtype=jnp.int32)[None, None, :]
    filled = slot_index < route_count[:, :, None]
    allowed = (slot_index < CAP_HOME) | (copy_plan[None, :, None] == 1)
    weights = jnp.where(filled & allowed, route_prob, jnp.zeros_like(route_prob))
    source_base = (jnp.arange(N_EXPERT, dtype=jnp.int32) * TOK_DEV)[:, None, None]
    global_token = (route_token + source_base).astype(jnp.int32)
    token_by_expert = jnp.transpose(global_token, (1, 0, 2))
    weight_by_expert = jnp.transpose(weights, (1, 0, 2))

    def one_expert(inputs):
        token_ids, slot_weights, weight_in, weight_out = inputs
        flat_ids = token_ids.reshape(-1)
        picked = tokens[flat_ids]
        scaled = (slot_weights.reshape(-1, 1) * cotangent[flat_ids].astype(jnp.float32)).astype(jnp.bfloat16)
        preact = jnp.dot(picked, weight_in, preferred_element_type=jnp.float32)
        hidden = jax.nn.silu(preact).astype(jnp.bfloat16)
        expert_rows = jnp.dot(hidden, weight_out, preferred_element_type=jnp.float32)
        hidden_grad = jnp.dot(scaled, weight_out.T, preferred_element_type=jnp.float32)
        pre_grad = (hidden_grad * silu_slope(preact)).astype(jnp.bfloat16)
        input_rows = jnp.dot(pre_grad, weight_in.T, preferred_element_type=jnp.float32)
        grad_in = jnp.dot(picked.T, pre_grad, preferred_element_type=jnp.float32).astype(jnp.bfloat16)
        grad_out = jnp.dot(hidden.T, scaled, preferred_element_type=jnp.float32).astype(jnp.bfloat16)
        return expert_rows, input_rows, grad_in, grad_out

    expert_rows, input_rows, w_in_grad, w_out_grad = lax.map(one_expert, (token_by_expert, weight_by_expert, w_in, w_out))
    flat_ids = token_by_expert.reshape(-1).astype(jnp.int32)
    weighted = expert_rows * weight_by_expert.reshape(EXPERTS, -1, 1)
    expert_out = jax.ops.segment_sum(weighted.reshape(-1, D), flat_ids, num_segments=TOKENS).astype(jnp.bfloat16)
    token_grad = jax.ops.segment_sum(input_rows.reshape(-1, D), flat_ids, num_segments=TOKENS).astype(jnp.bfloat16)
    return expert_out, token_grad, w_in_grad, w_out_grad
```

```python
import functools
import math

import jax
import jax.numpy as jnp
from jax import lax
from jax.experimental import pallas as pl
from jax.experimental.pallas import tpu as pltpu
from jax.sharding import PartitionSpec as P

F32 = jnp.float32
BF16 = jnp.bfloat16
MESH = pl.DeviceIdType.MESH
CHUNKS = 4
SKEW = 1


def dot(a, b, ca, cb, precision=None):
    return lax.dot_general(
        a, b, (((ca,), (cb,)), ((), ())), precision=precision, preferred_element_type=F32
    )


def iota(shape, axis):
    return lax.broadcasted_iota(jnp.int32, shape, axis)


def moe_kernel(
    experts,
    zs,
    tok_ref,
    cot_ref,
    w_in_ref,
    w_out_ref,
    route_ref,
    count_ref,
    plan_ref,
    prob_ref,
    out_ref,
    tgrad_ref,
    gin_ref,
    gout_ref,
    send_buf,
    recv_buf,
    rows_buf,
    scaled_buf,
    pair_send,
    pair_recv,
    part_buf,
    rs_send,
    rs_recv,
    act_buf,
    ret_send,
    ret_recv,
    comb_buf,
    a2a_send_sem,
    a2a_recv_sem,
    pair_send_sem,
    pair_recv_sem,
    rs_send_sem,
    rs_recv_sem,
    ag_send_sem,
    ag_recv_sem,
    sib_send_sem,
    sib_recv_sem,
    ret_send_sem,
    ret_recv_sem,
):
    cap = route_ref.shape[0]
    half_cap = cap // 2
    width, tokens = tok_ref.shape
    hidden = w_in_ref.shape[1]
    half = hidden // 2
    slots = experts * cap
    chunk_rows = slots // CHUNKS
    chunk_blocks = experts // CHUNKS
    own_rows = chunk_rows // zs
    far, near = zs // 2, zs - 1 - zs // 2
    nx = math.isqrt(experts)
    ny = experts // nx

    me = lax.axis_index("expert")
    my_y, my_x = me // nx, me % nx
    dp = lax.axis_index("dp")
    z, core = dp // 2, dp % 2
    other = 1 - core
    sibling = {"dp": z * 2 + other}
    turn = 1 - 2 * core
    ahead = {"dp": ((z + turn + zs) % zs) * 2 + core}
    behind = {"dp": ((z - turn + zs) % zs) * 2 + core}

    def offset(j):
        return (3 * (j // nx)) % ny, j % nx

    def to_expert(j):
        dy, dx = offset(j)
        return ((my_y + dy) % ny) * nx + (my_x + dx) % nx

    def from_expert(j):
        dy, dx = offset(j)
        return ((my_y - dy + ny) % ny) * nx + (my_x - dx + nx) % nx

    def owner(steps):
        return (z + turn * steps + 2 * zs) % zs

    def remote(src, dst, send_sem, recv_sem, device):
        return pltpu.make_async_remote_copy(
            src_ref=src,
            dst_ref=dst,
            send_sem=send_sem,
            recv_sem=recv_sem,
            device_id=device,
            device_id_type=MESH,
        )

    barrier = pltpu.get_barrier_semaphore()

    def greet(j, carry):
        pl.semaphore_signal(
            barrier, inc=1, device_id={"expert": to_expert(j)}, device_id_type=MESH
        )
        return carry

    lax.fori_loop(1, experts, greet, 0)
    for device in (sibling, ahead, behind):
        pl.semaphore_signal(barrier, inc=1, device_id=device, device_id_type=MESH)

    slot = iota((cap, experts), 0)
    used = (slot < count_ref[...]) & ((slot < half_cap) | (plan_ref[...] == 1))
    weights = jnp.where(used, prob_ref[...], 0.0)
    spread = (iota((slots, experts), 0) // cap == iota((slots, experts), 1)).astype(F32)
    mine = iota((slots, cap), 0) % cap == iota((slots, cap), 1)

    def as_column(table):
        wide = dot(spread, table, 1, 1, lax.Precision.HIGHEST)
        return jnp.sum(jnp.where(mine, wide, 0.0), axis=1, keepdims=True)

    token_col = as_column(route_ref[...].astype(F32))
    weight_col = as_column(weights)
    hot = (token_col == iota((slots, tokens), 1).astype(F32)).astype(F32)
    hot16 = hot.astype(BF16)
    picked = dot(hot16, tok_ref[...], 1, 1).reshape(experts, cap, width)
    scaled = (weight_col * dot(hot16, cot_ref[...], 1, 1)).reshape(experts, cap, width)
    send_buf[...] = jnp.concatenate([picked, scaled], axis=1).astype(BF16)

    pl.semaphore_wait(barrier, experts - 1 + 3)

    def dispatch(j, carry):
        e = to_expert(j)
        remote(
            send_buf.at[e],
            recv_buf.at[j],
            a2a_send_sem,
            a2a_recv_sem.at[j // chunk_blocks],
            {"expert": e},
        ).start()
        return carry

    lax.fori_loop(1, experts, dispatch, 0)
    recv_buf[0] = send_buf[me]

    weighted = (hot * weight_col).T
    weighted_hi = weighted.astype(BF16)
    comb_buf[0] = weighted_hi
    comb_buf[1] = (weighted - weighted_hi.astype(F32)).astype(BF16)
    comb_buf[2] = hot.T.astype(BF16)

    def chunk_slice(k):
        return pl.ds(k * chunk_rows, chunk_rows)

    def share_rows(k, steps):
        start = pl.multiple_of(k * chunk_rows + owner(steps) * own_rows, own_rows)
        return pl.ds(start, own_rows)

    def part_of(k, steps):
        start = pl.multiple_of(owner(steps) * own_rows, own_rows)
        return part_buf[k, :, pl.ds(start, own_rows), :]

    def pair_copy(k):
        return remote(
            pair_send.at[k],
            pair_recv.at[k],
            pair_send_sem.at[k],
            pair_recv_sem.at[k],
            sibling,
        )

    def rs_copy(k, n):
        return remote(
            rs_send.at[k, n],
            rs_recv.at[k, n],
            rs_send_sem.at[k, n],
            rs_recv_sem.at[k, n],
            ahead if n < far else behind,
        )

    def ag_copy(k, n):
        s = -n if n < far else n - far
        place = act_buf.at[core, :, share_rows(k, s), :]
        return remote(
            place,
            place,
            ag_send_sem.at[k, n],
            ag_recv_sem.at[k, n],
            ahead if n < far else behind,
        )

    def sib_copy(k, steps, n):
        place = act_buf.at[core, :, share_rows(k, steps), :]
        return remote(place, place, sib_send_sem.at[k, n], sib_recv_sem.at[k], sibling)

    def partials(k):
        first = 1 if k == 0 else 0
        blocks = recv_buf.at[pl.ds(k * chunk_blocks + first, chunk_blocks - first)]
        remote(blocks, blocks, a2a_send_sem, a2a_recv_sem.at[k], sibling).wait_recv()
        both = recv_buf[pl.ds(k * chunk_blocks, chunk_blocks)].astype(F32)
        rows = both[:, :cap].reshape(chunk_rows, width).astype(BF16)
        grads = both[:, cap:].reshape(chunk_rows, width).astype(BF16)
        rows_buf[chunk_slice(k), :] = rows
        scaled_buf[chunk_slice(k), :] = grads
        pre = dot(rows, w_in_ref[...], 1, 0)
        grad = dot(grads, w_out_ref[...], 1, 0)
        low = core == 0
        part_buf[k, 0] = jnp.where(low, pre[:, :half], pre[:, half:])
        part_buf[k, 1] = jnp.where(low, grad[:, :half], grad[:, half:])
        pair_send[k, 0] = jnp.where(low, pre[:, half:], pre[:, :half]).astype(BF16)
        pair_send[k, 1] = jnp.where(low, grad[:, half:], grad[:, :half]).astype(BF16)
        pair_copy(k).start()

    def rs_start(k):
        pair_copy(k).wait_recv()
        part_buf[k] = part_buf[k] + pair_recv[k].astype(F32)
        rs_send[k, 0] = part_of(k, far).astype(BF16)
        rs_copy(k, 0).start()
        rs_send[k, far] = part_of(k, -near).astype(BF16)
        rs_copy(k, far).start()

    def rs_step(k, s):
        for base, length, sign in ((0, far, 1), (far, near, -1)):
            if s < length:
                n = base + s
                rs_copy(k, n - 1).wait_recv()
                mixed = part_of(k, sign * (length - s)) + rs_recv[k, n - 1].astype(F32)
                rs_send[k, n] = mixed.astype(BF16)
                rs_copy(k, n).start()

    def activate(k):
        rs_copy(k, far - 1).wait_recv()
        total = part_of(k, 0) + rs_recv[k, far - 1].astype(F32)
        rs_copy(k, far + near - 1).wait_recv()
        total = total + rs_recv[k, far + near - 1].astype(F32)
        pre, grad = total[0], total[1]
        gate = 1.0 / (1.0 + jnp.exp(-pre))
        act_buf[core, 0, share_rows(k, 0), :] = (pre * gate).astype(BF16)
        slope = gate * (1.0 + pre * (1.0 - gate))
        act_buf[core, 1, share_rows(k, 0), :] = (grad * slope).astype(BF16)
        ag_copy(k, 0).start()
        ag_copy(k, far).start()
        sib_copy(k, 0, 0).start()

    def ag_step(k, s):
        for base, length, sign in ((0, far, -1), (far, near, 1)):
            if s <= length:
                ag_came(k, base + s - 1, sign * s)
                if s < length:
                    ag_copy(k, base + s).start()
                sib_copy(k, sign * s, base + s if base == 0 else far + s).start()

    def ag_came(k, n, steps):
        place = act_buf.at[core, :, share_rows(k, steps), :]
        remote(place, place, ag_send_sem.at[k, n], ag_recv_sem.at[k, n], sibling).wait_recv()

    def returns(k):
        place = act_buf.at[other, :, chunk_slice(k), :]
        remote(place, place, sib_send_sem.at[k, 0], sib_recv_sem.at[k], sibling).wait_recv()
        rows = chunk_slice(k)
        out_rows = dot(act_buf[0, 0, rows, :], w_out_ref[:, :half], 1, 1)
        out_rows = out_rows + dot(act_buf[1, 0, rows, :], w_out_ref[:, half:], 1, 1)
        in_rows = dot(act_buf[0, 1, rows, :], w_in_ref[:, :half], 1, 1)
        in_rows = in_rows + dot(act_buf[1, 1, rows, :], w_in_ref[:, half:], 1, 1)
        ret_send[pl.ds(k * chunk_blocks, chunk_blocks)] = jnp.concatenate(
            [
                out_rows.reshape(chunk_blocks, cap, width),
                in_rows.reshape(chunk_blocks, cap, width),
            ],
            axis=1,
        ).astype(BF16)
        if k == 0:
            ret_recv[me] = ret_send[0]

        def give_back(j, carry):
            remote(
                ret_send.at[j],
                ret_recv.at[me],
                ret_send_sem,
                ret_recv_sem,
                {"expert": from_expert(j)},
            ).start()
            return carry

        first = 1 if k == 0 else 0
        lax.fori_loop(k * chunk_blocks + first, (k + 1) * chunk_blocks, give_back, 0)

    stages = [partials, rs_start]
    for s in range(1, far):
        stages.append(functools.partial(lambda k, s: rs_step(k, s), s=s))
    stages.append(activate)
    for s in range(1, far + 1):
        stages.append(functools.partial(lambda k, s: ag_step(k, s), s=s))
    stages.append(returns)
    for t in range(len(stages) + SKEW * (CHUNKS - 1)):
        for k in range(CHUNKS):
            if 0 <= t - SKEW * k < len(stages):
                stages[t - SKEW * k](k)

    for h in range(2):
        cols = pl.ds(h * half, half)
        gin_ref[:, cols] = dot(rows_buf[...], act_buf[h, 1], 0, 0).astype(BF16)
        gout_ref[:, cols] = dot(scaled_buf[...], act_buf[h, 0], 0, 0).astype(BF16)

    blocks = ret_recv.at[pl.ds(0, experts - 1)]
    remote(blocks, blocks, ret_send_sem, ret_recv_sem, sibling).wait_recv()
    both = ret_recv[...].astype(F32)
    out_rows = both[:, :cap].reshape(slots, width).astype(BF16)
    in_rows = both[:, cap:].reshape(slots, width).astype(BF16)
    sums = dot(comb_buf[0], out_rows, 1, 0) + dot(comb_buf[1], out_rows, 1, 0)
    out_ref[...] = sums.T.astype(BF16)
    tgrad_ref[...] = dot(comb_buf[2], in_rows, 1, 0).T.astype(BF16)

    blocks = send_buf.at[pl.ds(0, experts - 1)]
    remote(blocks, blocks, a2a_send_sem, a2a_recv_sem.at[0], sibling).wait_send()
    blocks = ret_send.at[pl.ds(1, experts - 1)]
    remote(blocks, blocks, ret_send_sem, ret_recv_sem, sibling).wait_send()
    for k in range(CHUNKS):
        pair_copy(k).wait_send()
        for n in range(far + near):
            rs_copy(k, n).wait_send()
            ag_copy(k, n).wait_send()
        for n in range(zs):
            sib_copy(k, 0, n).wait_send()


def on_device(tokens, cotangent, w_in, w_out, route_token, route_count, copy_plan, route_prob):
    experts, cap = route_token.shape[1:]
    zs = lax.axis_size("dp") // 2
    count, width = tokens.shape
    hidden = w_in.shape[2]
    half = hidden // 2
    slots = experts * cap
    chunk_rows = slots // CHUNKS
    own_rows = chunk_rows // zs
    vmem = pl.BlockSpec(memory_space=pltpu.VMEM)
    dma = pltpu.SemaphoreType.DMA
    out, tgrad, gin, gout = pl.pallas_call(
        functools.partial(moe_kernel, experts, zs),
        out_shape=(
            jax.ShapeDtypeStruct((width, count), BF16),
            jax.ShapeDtypeStruct((width, count), BF16),
            jax.ShapeDtypeStruct((width, hidden), BF16),
            jax.ShapeDtypeStruct((width, hidden), BF16),
        ),
        in_specs=[vmem] * 8,
        out_specs=(vmem,) * 4,
        scratch_shapes=[
            pltpu.VMEM((experts, 2 * cap, width), BF16),
            pltpu.VMEM((experts, 2 * cap, width), BF16),
            pltpu.VMEM((slots, width), BF16),
            pltpu.VMEM((slots, width), BF16),
            pltpu.VMEM((CHUNKS, 2, chunk_rows, half), BF16),
            pltpu.VMEM((CHUNKS, 2, chunk_rows, half), BF16),
            pltpu.VMEM((CHUNKS, 2, chunk_rows, half), F32),
            pltpu.VMEM((CHUNKS, zs - 1, 2, own_rows, half), BF16),
            pltpu.VMEM((CHUNKS, zs - 1, 2, own_rows, half), BF16),
            pltpu.VMEM((2, 2, slots, half), BF16),
            pltpu.VMEM((experts, 2 * cap, width), BF16),
            pltpu.VMEM((experts, 2 * cap, width), BF16),
            pltpu.VMEM((3, count, slots), BF16),
            dma,
            dma((CHUNKS,)),
            dma((CHUNKS,)),
            dma((CHUNKS,)),
            dma((CHUNKS, zs - 1)),
            dma((CHUNKS, zs - 1)),
            dma((CHUNKS, zs - 1)),
            dma((CHUNKS, zs - 1)),
            dma((CHUNKS, zs)),
            dma((CHUNKS,)),
            dma,
            dma,
        ],
        compiler_params=pltpu.CompilerParams(
            collective_id=0, has_side_effects=True, vmem_limit_bytes=40 << 20
        ),
        name="moe_layer",
    )(
        tokens.T,
        cotangent.T,
        w_in[0],
        w_out[0].T,
        route_token[0].T,
        route_count,
        copy_plan[None],
        route_prob[0].T,
    )
    return out.T, tgrad.T, gin[None], gout.T[None]


def solution(mesh):
    in_specs = (
        P("expert", "dp"),
        P("expert", "dp"),
        P("expert", "dp", None),
        P("expert", None, "dp"),
        P("expert", None, None),
        P("expert", None),
        P(),
        P("expert", None, None),
    )
    out_specs = (
        P("expert", "dp"),
        P("expert", "dp"),
        P("expert", "dp", None),
        P("expert", None, "dp"),
    )
    return jax.shard_map(
        on_device, mesh=mesh, in_specs=in_specs, out_specs=out_specs, check_vma=False
    )
```

```python
import functools
import math

import jax
import jax.numpy as jnp
from jax import lax
from jax.experimental import pallas as pl
from jax.experimental.pallas import tpu as pltpu
from jax.sharding import PartitionSpec as P

F32 = jnp.float32
BF16 = jnp.bfloat16
MESH = pl.DeviceIdType.MESH
CHUNKS = 4
STARTS = (0, 1, 2, 3)
FLIGHT = 4


def dot(a, b, ca, cb, precision=None):
    return lax.dot_general(
        a, b, (((ca,), (cb,)), ((), ())), precision=precision, preferred_element_type=F32
    )


def iota(shape, axis):
    return lax.broadcasted_iota(jnp.int32, shape, axis)


def offsets(ny, nx):
    def hops(o):
        return min(o[0], ny - o[0]) + min(o[1], nx - o[1])

    near = sorted(((dy, dx) for dy in range(ny) for dx in range(nx)), key=hops)
    size = len(near) // CHUNKS
    return near[:size] + near[2 * size :] + near[size : 2 * size] if CHUNKS > 1 else near


def moe_kernel(
    experts,
    zs,
    tok_hbm,
    cot_hbm,
    w_in_hbm,
    w_out_hbm,
    route_hbm,
    count_hbm,
    plan_hbm,
    prob_hbm,
    offset_hbm,
    out_hbm,
    tgrad_hbm,
    gin_hbm,
    gout_hbm,
    tok_ref,
    cot_ref,
    w_in_ref,
    w_out_ref,
    route_ref,
    count_ref,
    plan_ref,
    prob_ref,
    offset_ref,
    send_buf,
    recv_buf,
    rows_buf,
    scaled_buf,
    pair_send,
    pair_recv,
    part_buf,
    rs_send,
    rs_recv,
    act_buf,
    ret_send,
    ret_recv,
    comb_buf,
    sums_buf,
    out_ref,
    tgrad_ref,
    gin_ref,
    gout_ref,
    load_sem,
    store_sem,
    a2a_send_sem,
    a2a_recv_sem,
    pair_send_sem,
    pair_recv_sem,
    rs_send_sem,
    rs_recv_sem,
    ag_send_sem,
    ag_recv_sem,
    sib_send_sem,
    sib_recv_sem,
    ret_send_sem,
    ret_recv_sem,
):
    cap = route_ref.shape[0]
    half_cap = cap // 2
    width, tokens = tok_ref.shape
    hidden = w_in_ref.shape[1]
    half = hidden // 2
    slots = experts * cap
    chunk_rows = slots // CHUNKS
    chunk_blocks = experts // CHUNKS
    own_rows = chunk_rows // zs
    far, near = zs // 2, zs - 1 - zs // 2
    nx = math.isqrt(experts)
    ny = experts // nx

    me = lax.axis_index("expert")
    my_y, my_x = me // nx, me % nx
    dp = lax.axis_index("dp")
    z, core = dp // 2, dp % 2
    other = 1 - core
    sibling = {"dp": z * 2 + other}
    turn = 1 - 2 * core
    ahead = {"dp": ((z + turn + zs) % zs) * 2 + core}
    behind = {"dp": ((z - turn + zs) % zs) * 2 + core}

    places = offsets(ny, nx)

    def to_expert(j):
        dy, dx = places[j]
        return ((my_y + dy) % ny) * nx + (my_x + dx) % nx

    def from_expert(j):
        dy, dx = places[j]
        return ((my_y - dy + ny) % ny) * nx + (my_x - dx + nx) % nx

    def owner(steps):
        return (z + turn * steps + 2 * zs) % zs

    def remote(src, dst, send_sem, recv_sem, device):
        return pltpu.make_async_remote_copy(
            src_ref=src,
            dst_ref=dst,
            send_sem=send_sem,
            recv_sem=recv_sem,
            device_id=device,
            device_id_type=MESH,
        )

    pairs = (
        (route_hbm, route_ref),
        (count_hbm, count_ref),
        (plan_hbm, plan_ref),
        (prob_hbm, prob_ref),
        (offset_hbm, offset_ref),
        (tok_hbm, tok_ref),
        (cot_hbm, cot_ref),
        (w_in_hbm, w_in_ref),
        (w_out_hbm, w_out_ref),
    )
    loads = [pltpu.make_async_copy(a, b, load_sem.at[i]) for i, (a, b) in enumerate(pairs)]
    for load in loads:
        load.start()

    barrier = pltpu.get_barrier_semaphore()

    def distance(j):
        dy, dx = places[j]
        return min(dy, ny - dy) + min(dx, nx - dx)

    for j in sorted(range(1, experts), key=distance, reverse=True):
        pl.semaphore_signal(
            barrier, inc=1, device_id={"expert": to_expert(j)}, device_id_type=MESH
        )
    for device in (sibling, ahead, behind):
        pl.semaphore_signal(barrier, inc=1, device_id=device, device_id_type=MESH)

    for load in loads[:5]:
        load.wait()
    slot = iota((cap, experts), 0)
    used = (slot < count_ref[...]) & ((slot < half_cap) | (plan_ref[...] == 1))
    weights = jnp.where(used, prob_ref[...], 0.0)
    spread = (iota((slots, experts), 0) // cap == iota((slots, experts), 1)).astype(F32)
    there_y = (offset_ref[0:1, :] + my_y) % ny
    there_x = (offset_ref[1:2, :] + my_x) % nx
    order = (iota((experts, experts), 0) == there_y * nx + there_x).astype(F32)
    mine = iota((slots, cap), 0) % cap == iota((slots, cap), 1)

    def as_column(table):
        table = dot(table, order, 1, 0, lax.Precision.HIGHEST)
        wide = dot(spread, table, 1, 1, lax.Precision.HIGHEST)
        return jnp.sum(jnp.where(mine, wide, 0.0), axis=1, keepdims=True)

    token_col = as_column(route_ref[...].astype(F32))
    weight_col = as_column(weights)
    hot = (token_col == iota((slots, tokens), 1).astype(F32)).astype(F32)
    hot16 = hot.astype(BF16)
    for load in loads[5:7]:
        load.wait()
    picked = dot(hot16, tok_ref[...], 1, 1).reshape(experts, cap, width)
    scaled = (weight_col * dot(hot16, cot_ref[...], 1, 1)).reshape(experts, cap, width)
    send_buf[...] = jnp.concatenate([picked, scaled], axis=1).astype(BF16)

    pl.semaphore_wait(barrier, experts - 1 + 3)

    def dispatch_chunk(k):
        for j in range(max(1, k * chunk_blocks), (k + 1) * chunk_blocks):
            remote(
                send_buf.at[j],
                recv_buf.at[j],
                a2a_send_sem,
                a2a_recv_sem.at[k],
                {"expert": to_expert(j)},
            ).start()

    for k in range(FLIGHT):
        dispatch_chunk(k)
    recv_buf[0] = send_buf[0]

    weighted = (hot * weight_col).T
    weighted_hi = weighted.astype(BF16)
    comb_buf[0] = weighted_hi
    comb_buf[1] = (weighted - weighted_hi.astype(F32)).astype(BF16)
    comb_buf[2] = hot.T.astype(BF16)
    for load in loads[7:]:
        load.wait()

    def chunk_slice(k):
        return pl.ds(k * chunk_rows, chunk_rows)

    def share_rows(k, steps):
        start = pl.multiple_of(k * chunk_rows + owner(steps) * own_rows, own_rows)
        return pl.ds(start, own_rows)

    def part_of(k, steps):
        start = pl.multiple_of(owner(steps) * own_rows, own_rows)
        return part_buf[k, :, pl.ds(start, own_rows), :]

    def pair_copy(k):
        return remote(
            pair_send.at[k],
            pair_recv.at[k],
            pair_send_sem.at[k],
            pair_recv_sem.at[k],
            sibling,
        )

    def rs_copy(k, n):
        return remote(
            rs_send.at[k, n],
            rs_recv.at[k, n],
            rs_send_sem.at[k, n],
            rs_recv_sem.at[k, n],
            ahead if n < far else behind,
        )

    def ag_copy(k, n):
        s = -n if n < far else n - far
        place = act_buf.at[core, :, share_rows(k, s), :]
        return remote(
            place,
            place,
            ag_send_sem.at[k, n],
            ag_recv_sem.at[k, n],
            ahead if n < far else behind,
        )

    def sib_copy(k, steps, n):
        place = act_buf.at[core, :, share_rows(k, steps), :]
        return remote(place, place, sib_send_sem.at[k, n], sib_recv_sem.at[k], sibling)

    def partials(k):
        first = 1 if k == 0 else 0
        blocks = recv_buf.at[pl.ds(k * chunk_blocks + first, chunk_blocks - first)]
        remote(blocks, blocks, a2a_send_sem, a2a_recv_sem.at[k], sibling).wait_recv()
        if k + FLIGHT < CHUNKS:
            dispatch_chunk(k + FLIGHT)
        both = recv_buf[pl.ds(k * chunk_blocks, chunk_blocks)].astype(F32)
        rows = both[:, :cap].reshape(chunk_rows, width).astype(BF16)
        grads = both[:, cap:].reshape(chunk_rows, width).astype(BF16)
        rows_buf[chunk_slice(k), :] = rows
        scaled_buf[chunk_slice(k), :] = grads
        pre = dot(rows, w_in_ref[...], 1, 0)
        grad = dot(grads, w_out_ref[...], 1, 0)
        low = core == 0
        part_buf[k, 0] = jnp.where(low, pre[:, :half], pre[:, half:])
        part_buf[k, 1] = jnp.where(low, grad[:, :half], grad[:, half:])
        pair_send[k, 0] = jnp.where(low, pre[:, half:], pre[:, :half]).astype(BF16)
        pair_send[k, 1] = jnp.where(low, grad[:, half:], grad[:, :half]).astype(BF16)
        pair_copy(k).start()

    def rs_start(k):
        pair_copy(k).wait_recv()
        part_buf[k] = part_buf[k] + pair_recv[k].astype(F32)
        rs_send[k, 0] = part_of(k, far).astype(BF16)
        rs_copy(k, 0).start()
        rs_send[k, far] = part_of(k, -near).astype(BF16)
        rs_copy(k, far).start()

    def rs_step(k, s):
        for base, length, sign in ((0, far, 1), (far, near, -1)):
            if s < length:
                n = base + s
                rs_copy(k, n - 1).wait_recv()
                mixed = part_of(k, sign * (length - s)) + rs_recv[k, n - 1].astype(F32)
                rs_send[k, n] = mixed.astype(BF16)
                rs_copy(k, n).start()

    def activate(k):
        rs_copy(k, far - 1).wait_recv()
        total = part_of(k, 0) + rs_recv[k, far - 1].astype(F32)
        rs_copy(k, far + near - 1).wait_recv()
        total = total + rs_recv[k, far + near - 1].astype(F32)
        pre, grad = total[0], total[1]
        gate = 1.0 / (1.0 + jnp.exp(-pre))
        act_buf[core, 0, share_rows(k, 0), :] = (pre * gate).astype(BF16)
        slope = gate * (1.0 + pre * (1.0 - gate))
        act_buf[core, 1, share_rows(k, 0), :] = (grad * slope).astype(BF16)
        ag_copy(k, 0).start()
        ag_copy(k, far).start()
        sib_copy(k, 0, 0).start()

    def ag_step(k, s):
        for base, length, sign in ((0, far, -1), (far, near, 1)):
            if s <= length:
                ag_came(k, base + s - 1, sign * s)
                if s < length:
                    ag_copy(k, base + s).start()
                sib_copy(k, sign * s, base + s if base == 0 else far + s).start()

    def ag_came(k, n, steps):
        place = act_buf.at[core, :, share_rows(k, steps), :]
        remote(place, place, ag_send_sem.at[k, n], ag_recv_sem.at[k, n], sibling).wait_recv()

    def returns(k):
        place = act_buf.at[other, :, chunk_slice(k), :]
        remote(place, place, sib_send_sem.at[k, 0], sib_recv_sem.at[k], sibling).wait_recv()
        rows = chunk_slice(k)
        out_rows = dot(act_buf[0, 0, rows, :], w_out_ref[:, :half], 1, 1)
        out_rows = out_rows + dot(act_buf[1, 0, rows, :], w_out_ref[:, half:], 1, 1)
        in_rows = dot(act_buf[0, 1, rows, :], w_in_ref[:, :half], 1, 1)
        in_rows = in_rows + dot(act_buf[1, 1, rows, :], w_in_ref[:, half:], 1, 1)
        ret_send[pl.ds(k * chunk_blocks, chunk_blocks)] = jnp.concatenate(
            [
                out_rows.reshape(chunk_blocks, cap, width),
                in_rows.reshape(chunk_blocks, cap, width),
            ],
            axis=1,
        ).astype(BF16)
        if k == 0:
            ret_recv[0] = ret_send[0]

        for j in range(max(1, k * chunk_blocks), (k + 1) * chunk_blocks):
            remote(
                ret_send.at[j],
                ret_recv.at[j],
                ret_send_sem,
                ret_recv_sem.at[k],
                {"expert": from_expert(j)},
            ).start()

    stages = [partials, rs_start]
    for s in range(1, far):
        stages.append(functools.partial(lambda k, s: rs_step(k, s), s=s))
    stages.append(activate)
    for s in range(1, far + 1):
        stages.append(functools.partial(lambda k, s: ag_step(k, s), s=s))
    stages.append(returns)
    steps = [(n + STARTS[k], k, n) for k in range(CHUNKS) for n in range(len(stages))]
    for _, k, n in sorted(steps):
        stages[n](k)

    for h in range(2):
        cols = pl.ds(h * half, half)
        gin_ref[:, cols] = dot(rows_buf[...], act_buf[h, 1], 0, 0).astype(BF16)
        gout_ref[:, cols] = dot(scaled_buf[...], act_buf[h, 0], 0, 0).astype(BF16)

    pairs = ((out_ref, out_hbm), (tgrad_ref, tgrad_hbm), (gin_ref, gin_hbm), (gout_ref, gout_hbm))
    stores = [pltpu.make_async_copy(a, b, store_sem.at[i]) for i, (a, b) in enumerate(pairs)]
    stores[2].start()
    stores[3].start()

    for k in range(CHUNKS):
        first = 1 if k == 0 else 0
        blocks = ret_recv.at[pl.ds(k * chunk_blocks + first, chunk_blocks - first)]
        remote(blocks, blocks, ret_send_sem, ret_recv_sem.at[k], sibling).wait_recv()
        both = ret_recv[pl.ds(k * chunk_blocks, chunk_blocks)].astype(F32)
        out_rows = both[:, :cap].reshape(chunk_rows, width).astype(BF16)
        in_rows = both[:, cap:].reshape(chunk_rows, width).astype(BF16)
        cols = chunk_slice(k)
        sums = dot(comb_buf[0, :, cols], out_rows, 1, 0)
        sums = sums + dot(comb_buf[1, :, cols], out_rows, 1, 0)
        grads = dot(comb_buf[2, :, cols], in_rows, 1, 0)
        if k > 0:
            sums, grads = sums_buf[0] + sums, sums_buf[1] + grads
        if k < CHUNKS - 1:
            sums_buf[0] = sums
            sums_buf[1] = grads
        else:
            out_ref[...] = sums.T.astype(BF16)
            tgrad_ref[...] = grads.T.astype(BF16)

    stores[0].start()
    stores[1].start()

    blocks = send_buf.at[pl.ds(0, experts - 1)]
    remote(blocks, blocks, a2a_send_sem, a2a_recv_sem.at[0], sibling).wait_send()
    blocks = ret_send.at[pl.ds(1, experts - 1)]
    remote(blocks, blocks, ret_send_sem, ret_recv_sem.at[0], sibling).wait_send()
    for k in range(CHUNKS):
        pair_copy(k).wait_send()
        for n in range(far + near):
            rs_copy(k, n).wait_send()
            ag_copy(k, n).wait_send()
        for n in range(zs):
            sib_copy(k, 0, n).wait_send()
    for store in stores:
        store.wait()


def on_device(tokens, cotangent, w_in, w_out, route_token, route_count, copy_plan, route_prob):
    experts, cap = route_token.shape[1:]
    zs = lax.axis_size("dp") // 2
    nx = math.isqrt(experts)
    ny = experts // nx
    count, width = tokens.shape
    hidden = w_in.shape[2]
    half = hidden // 2
    slots = experts * cap
    chunk_rows = slots // CHUNKS
    own_rows = chunk_rows // zs
    hbm = pl.BlockSpec(memory_space=pltpu.HBM)
    dma = pltpu.SemaphoreType.DMA
    out, tgrad, gin, gout = pl.pallas_call(
        functools.partial(moe_kernel, experts, zs),
        out_shape=(
            jax.ShapeDtypeStruct((width, count), BF16),
            jax.ShapeDtypeStruct((width, count), BF16),
            jax.ShapeDtypeStruct((width, hidden), BF16),
            jax.ShapeDtypeStruct((width, hidden), BF16),
        ),
        in_specs=[hbm] * 9,
        out_specs=(hbm,) * 4,
        scratch_shapes=[
            pltpu.VMEM((width, count), BF16),
            pltpu.VMEM((width, count), BF16),
            pltpu.VMEM((width, hidden), BF16),
            pltpu.VMEM((width, hidden), BF16),
            pltpu.VMEM((cap, experts), jnp.int32),
            pltpu.VMEM((1, experts), jnp.int32),
            pltpu.VMEM((1, experts), jnp.int32),
            pltpu.VMEM((cap, experts), F32),
            pltpu.VMEM((2, experts), jnp.int32),
            pltpu.VMEM((experts, 2 * cap, width), BF16),
            pltpu.VMEM((experts, 2 * cap, width), BF16),
            pltpu.VMEM((slots, width), BF16),
            pltpu.VMEM((slots, width), BF16),
            pltpu.VMEM((CHUNKS, 2, chunk_rows, half), BF16),
            pltpu.VMEM((CHUNKS, 2, chunk_rows, half), BF16),
            pltpu.VMEM((CHUNKS, 2, chunk_rows, half), F32),
            pltpu.VMEM((CHUNKS, zs - 1, 2, own_rows, half), BF16),
            pltpu.VMEM((CHUNKS, zs - 1, 2, own_rows, half), BF16),
            pltpu.VMEM((2, 2, slots, half), BF16),
            pltpu.VMEM((experts, 2 * cap, width), BF16),
            pltpu.VMEM((experts, 2 * cap, width), BF16),
            pltpu.VMEM((3, count, slots), BF16),
            pltpu.VMEM((2, count, width), F32),
            pltpu.VMEM((width, count), BF16),
            pltpu.VMEM((width, count), BF16),
            pltpu.VMEM((width, hidden), BF16),
            pltpu.VMEM((width, hidden), BF16),
            dma((9,)),
            dma((4,)),
            dma,
            dma((CHUNKS,)),
            dma((CHUNKS,)),
            dma((CHUNKS,)),
            dma((CHUNKS, zs - 1)),
            dma((CHUNKS, zs - 1)),
            dma((CHUNKS, zs - 1)),
            dma((CHUNKS, zs - 1)),
            dma((CHUNKS, zs)),
            dma((CHUNKS,)),
            dma,
            dma((CHUNKS,)),
        ],
        compiler_params=pltpu.CompilerParams(
            collective_id=0, has_side_effects=True, vmem_limit_bytes=60 << 20
        ),
        name="moe_layer",
    )(
        tokens.T,
        cotangent.T,
        w_in[0],
        w_out[0].T,
        route_token[0].T,
        route_count,
        copy_plan[None],
        route_prob[0].T,
        jnp.asarray(offsets(ny, nx), jnp.int32).T,
    )
    return out.T, tgrad.T, gin[None], gout.T[None]


def solution(mesh):
    in_specs = (
        P("expert", "dp"),
        P("expert", "dp"),
        P("expert", "dp", None),
        P("expert", None, "dp"),
        P("expert", None, None),
        P("expert", None),
        P(),
        P("expert", None, None),
    )
    out_specs = (
        P("expert", "dp"),
        P("expert", "dp"),
        P("expert", "dp", None),
        P("expert", None, "dp"),
    )
    return jax.shard_map(
        on_device, mesh=mesh, in_specs=in_specs, out_specs=out_specs, check_vma=False
    )
```

```python
import functools
import math

import jax
import jax.numpy as jnp
from jax import lax
from jax.experimental import pallas as pl
from jax.experimental.pallas import tpu as pltpu
from jax.sharding import PartitionSpec as P

F32 = jnp.float32
BF16 = jnp.bfloat16
MESH = pl.DeviceIdType.MESH
CHUNKS = 4
STARTS = (0, 1, 2, 3)
FLIGHT = 4


def dot(a, b, ca, cb, precision=None):
    return lax.dot_general(
        a, b, (((ca,), (cb,)), ((), ())), precision=precision, preferred_element_type=F32
    )


def iota(shape, axis):
    return lax.broadcasted_iota(jnp.int32, shape, axis)


def offsets(ny, nx):
    def hops(o):
        return min(o[0], ny - o[0]) + min(o[1], nx - o[1])

    near = sorted(((dy, dx) for dy in range(ny) for dx in range(nx)), key=hops)
    size = len(near) // CHUNKS
    return near[:size] + near[2 * size :] + near[size : 2 * size] if CHUNKS > 1 else near


def moe_kernel(
    experts,
    zs,
    tok_hbm,
    cot_hbm,
    w_in_hbm,
    w_out_hbm,
    route_hbm,
    count_hbm,
    plan_hbm,
    prob_hbm,
    offset_hbm,
    token_hbm,
    weight_hbm,
    tok_ref,
    cot_ref,
    w_in_ref,
    w_out_ref,
    route_ref,
    count_ref,
    plan_ref,
    prob_ref,
    offset_ref,
    send_buf,
    recv_buf,
    rows_buf,
    scaled_buf,
    pair_send,
    pair_recv,
    part_buf,
    rs_send,
    rs_recv,
    act_buf,
    ret_send,
    ret_recv,
    comb_buf,
    sums_buf,
    token_ref,
    weight_ref,
    load_sem,
    store_sem,
    a2a_send_sem,
    a2a_recv_sem,
    pair_send_sem,
    pair_recv_sem,
    rs_send_sem,
    rs_recv_sem,
    ag_send_sem,
    ag_recv_sem,
    sib_send_sem,
    sib_recv_sem,
    ret_send_sem,
    ret_recv_sem,
):
    cap = route_ref.shape[0]
    half_cap = cap // 2
    width, tokens = tok_ref.shape
    hidden = w_in_ref.shape[1]
    half = hidden // 2
    slots = experts * cap
    chunk_rows = slots // CHUNKS
    chunk_blocks = experts // CHUNKS
    own_rows = chunk_rows // zs
    far, near = zs // 2, zs - 1 - zs // 2
    nx = math.isqrt(experts)
    ny = experts // nx

    me = lax.axis_index("expert")
    my_y, my_x = me // nx, me % nx
    dp = lax.axis_index("dp")
    z, core = dp // 2, dp % 2
    other = 1 - core
    sibling = {"dp": z * 2 + other}
    turn = 1 - 2 * core
    ahead = {"dp": ((z + turn + zs) % zs) * 2 + core}
    behind = {"dp": ((z - turn + zs) % zs) * 2 + core}

    places = offsets(ny, nx)

    def to_expert(j):
        dy, dx = places[j]
        return ((my_y + dy) % ny) * nx + (my_x + dx) % nx

    def from_expert(j):
        dy, dx = places[j]
        return ((my_y - dy + ny) % ny) * nx + (my_x - dx + nx) % nx

    def owner(steps):
        return (z + turn * steps + 2 * zs) % zs

    def remote(src, dst, send_sem, recv_sem, device):
        return pltpu.make_async_remote_copy(
            src_ref=src,
            dst_ref=dst,
            send_sem=send_sem,
            recv_sem=recv_sem,
            device_id=device,
            device_id_type=MESH,
        )

    pairs = (
        (route_hbm, route_ref),
        (count_hbm, count_ref),
        (plan_hbm, plan_ref),
        (prob_hbm, prob_ref),
        (offset_hbm, offset_ref),
        (tok_hbm, tok_ref),
        (cot_hbm, cot_ref),
        (w_in_hbm, w_in_ref),
        (w_out_hbm, w_out_ref),
    )
    loads = [pltpu.make_async_copy(a, b, load_sem.at[i]) for i, (a, b) in enumerate(pairs)]
    for load in loads:
        load.start()

    barrier = pltpu.get_barrier_semaphore()

    def distance(j):
        dy, dx = places[j]
        return min(dy, ny - dy) + min(dx, nx - dx)

    for j in sorted(range(1, experts), key=distance, reverse=True):
        pl.semaphore_signal(
            barrier, inc=1, device_id={"expert": to_expert(j)}, device_id_type=MESH
        )
    for device in (sibling, ahead, behind):
        pl.semaphore_signal(barrier, inc=1, device_id=device, device_id_type=MESH)

    for load in loads[:5]:
        load.wait()
    slot = iota((cap, experts), 0)
    used = (slot < count_ref[...]) & ((slot < half_cap) | (plan_ref[...] == 1))
    weights = jnp.where(used, prob_ref[...], 0.0)
    spread = (iota((slots, experts), 0) // cap == iota((slots, experts), 1)).astype(F32)
    there_y = (offset_ref[0:1, :] + my_y) % ny
    there_x = (offset_ref[1:2, :] + my_x) % nx
    order = (iota((experts, experts), 0) == there_y * nx + there_x).astype(F32)
    mine = iota((slots, cap), 0) % cap == iota((slots, cap), 1)

    def as_column(table):
        table = dot(table, order, 1, 0, lax.Precision.HIGHEST)
        wide = dot(spread, table, 1, 1, lax.Precision.HIGHEST)
        return jnp.sum(jnp.where(mine, wide, 0.0), axis=1, keepdims=True)

    token_col = as_column(route_ref[...].astype(F32))
    weight_col = as_column(weights)
    hot = (token_col == iota((slots, tokens), 1).astype(F32)).astype(F32)
    hot16 = hot.astype(BF16)
    for load in loads[5:7]:
        load.wait()
    picked = dot(hot16, tok_ref[...], 1, 1).reshape(experts, cap, width)
    scaled = (weight_col * dot(hot16, cot_ref[...], 1, 1)).reshape(experts, cap, width)
    send_buf[...] = jnp.concatenate([picked, scaled], axis=1).astype(BF16)

    pl.semaphore_wait(barrier, experts - 1 + 3)

    def dispatch_chunk(k):
        for j in range(max(1, k * chunk_blocks), (k + 1) * chunk_blocks):
            remote(
                send_buf.at[j],
                recv_buf.at[j],
                a2a_send_sem,
                a2a_recv_sem.at[k],
                {"expert": to_expert(j)},
            ).start()

    for k in range(FLIGHT):
        dispatch_chunk(k)
    recv_buf[0] = send_buf[0]

    weighted = (hot * weight_col).T
    weighted_hi = weighted.astype(BF16)
    comb_buf[0] = weighted_hi
    comb_buf[1] = (weighted - weighted_hi.astype(F32)).astype(BF16)
    comb_buf[2] = hot.T.astype(BF16)
    for load in loads[7:]:
        load.wait()

    def chunk_slice(k):
        return pl.ds(k * chunk_rows, chunk_rows)

    def share_rows(k, steps):
        start = pl.multiple_of(k * chunk_rows + owner(steps) * own_rows, own_rows)
        return pl.ds(start, own_rows)

    def part_of(k, steps):
        start = pl.multiple_of(owner(steps) * own_rows, own_rows)
        return part_buf[k, :, pl.ds(start, own_rows), :]

    def pair_copy(k):
        return remote(
            pair_send.at[k],
            pair_recv.at[k],
            pair_send_sem.at[k],
            pair_recv_sem.at[k],
            sibling,
        )

    def rs_copy(k, n):
        return remote(
            rs_send.at[k, n],
            rs_recv.at[k, n],
            rs_send_sem.at[k, n],
            rs_recv_sem.at[k, n],
            ahead if n < far else behind,
        )

    def ag_copy(k, n):
        s = -n if n < far else n - far
        place = act_buf.at[core, :, share_rows(k, s), :]
        return remote(
            place,
            place,
            ag_send_sem.at[k, n],
            ag_recv_sem.at[k, n],
            ahead if n < far else behind,
        )

    def sib_copy(k, steps, n):
        place = act_buf.at[core, :, share_rows(k, steps), :]
        return remote(place, place, sib_send_sem.at[k, n], sib_recv_sem.at[k], sibling)

    def partials(k):
        first = 1 if k == 0 else 0
        blocks = recv_buf.at[pl.ds(k * chunk_blocks + first, chunk_blocks - first)]
        remote(blocks, blocks, a2a_send_sem, a2a_recv_sem.at[k], sibling).wait_recv()
        if k + FLIGHT < CHUNKS:
            dispatch_chunk(k + FLIGHT)
        both = recv_buf[pl.ds(k * chunk_blocks, chunk_blocks)].astype(F32)
        rows = both[:, :cap].reshape(chunk_rows, width).astype(BF16)
        grads = both[:, cap:].reshape(chunk_rows, width).astype(BF16)
        rows_buf[chunk_slice(k), :] = rows
        scaled_buf[chunk_slice(k), :] = grads
        pre = dot(rows, w_in_ref[...], 1, 0)
        grad = dot(grads, w_out_ref[...], 1, 0)
        low = core == 0
        part_buf[k, 0] = jnp.where(low, pre[:, :half], pre[:, half:])
        part_buf[k, 1] = jnp.where(low, grad[:, :half], grad[:, half:])
        pair_send[k, 0] = jnp.where(low, pre[:, half:], pre[:, :half]).astype(BF16)
        pair_send[k, 1] = jnp.where(low, grad[:, half:], grad[:, :half]).astype(BF16)
        pair_copy(k).start()

    def rs_start(k):
        pair_copy(k).wait_recv()
        part_buf[k] = part_buf[k] + pair_recv[k].astype(F32)
        rs_send[k, 0] = part_of(k, far).astype(BF16)
        rs_copy(k, 0).start()
        rs_send[k, far] = part_of(k, -near).astype(BF16)
        rs_copy(k, far).start()

    def rs_step(k, s):
        for base, length, sign in ((0, far, 1), (far, near, -1)):
            if s < length:
                n = base + s
                rs_copy(k, n - 1).wait_recv()
                mixed = part_of(k, sign * (length - s)) + rs_recv[k, n - 1].astype(F32)
                rs_send[k, n] = mixed.astype(BF16)
                rs_copy(k, n).start()

    def activate(k):
        rs_copy(k, far - 1).wait_recv()
        total = part_of(k, 0) + rs_recv[k, far - 1].astype(F32)
        rs_copy(k, far + near - 1).wait_recv()
        total = total + rs_recv[k, far + near - 1].astype(F32)
        pre, grad = total[0], total[1]
        gate = 1.0 / (1.0 + jnp.exp(-pre))
        act_buf[core, 0, share_rows(k, 0), :] = (pre * gate).astype(BF16)
        slope = gate * (1.0 + pre * (1.0 - gate))
        act_buf[core, 1, share_rows(k, 0), :] = (grad * slope).astype(BF16)
        ag_copy(k, 0).start()
        ag_copy(k, far).start()
        sib_copy(k, 0, 0).start()

    def ag_step(k, s):
        for base, length, sign in ((0, far, -1), (far, near, 1)):
            if s <= length:
                ag_came(k, base + s - 1, sign * s)
                if s < length:
                    ag_copy(k, base + s).start()
                sib_copy(k, sign * s, base + s if base == 0 else far + s).start()

    def ag_came(k, n, steps):
        place = act_buf.at[core, :, share_rows(k, steps), :]
        remote(place, place, ag_send_sem.at[k, n], ag_recv_sem.at[k, n], sibling).wait_recv()

    def returns(k):
        place = act_buf.at[other, :, chunk_slice(k), :]
        remote(place, place, sib_send_sem.at[k, 0], sib_recv_sem.at[k], sibling).wait_recv()
        rows = chunk_slice(k)
        out_rows = dot(act_buf[0, 0, rows, :], w_out_ref[:, :half], 1, 1)
        out_rows = out_rows + dot(act_buf[1, 0, rows, :], w_out_ref[:, half:], 1, 1)
        in_rows = dot(act_buf[0, 1, rows, :], w_in_ref[:, :half], 1, 1)
        in_rows = in_rows + dot(act_buf[1, 1, rows, :], w_in_ref[:, half:], 1, 1)
        ret_send[pl.ds(k * chunk_blocks, chunk_blocks)] = jnp.concatenate(
            [
                out_rows.reshape(chunk_blocks, cap, width),
                in_rows.reshape(chunk_blocks, cap, width),
            ],
            axis=1,
        ).astype(BF16)
        if k == 0:
            ret_recv[0] = ret_send[0]

        for j in range(max(1, k * chunk_blocks), (k + 1) * chunk_blocks):
            remote(
                ret_send.at[j],
                ret_recv.at[j],
                ret_send_sem,
                ret_recv_sem.at[k],
                {"expert": from_expert(j)},
            ).start()

    stages = [partials, rs_start]
    for s in range(1, far):
        stages.append(functools.partial(lambda k, s: rs_step(k, s), s=s))
    stages.append(activate)
    for s in range(1, far + 1):
        stages.append(functools.partial(lambda k, s: ag_step(k, s), s=s))
    stages.append(returns)
    steps = [(n + STARTS[k], k, n) for k in range(CHUNKS) for n in range(len(stages))]
    for _, k, n in sorted(steps):
        stages[n](k)

    for h in range(2):
        cols = pl.ds(h * half, half)
        weight_ref[0, :, cols] = dot(rows_buf[...], act_buf[h, 1], 0, 0)
        weight_ref[1, :, cols] = dot(scaled_buf[...], act_buf[h, 0], 0, 0)

    pairs = ((token_ref, token_hbm), (weight_ref, weight_hbm))
    stores = [pltpu.make_async_copy(a, b, store_sem.at[i]) for i, (a, b) in enumerate(pairs)]
    stores[1].start()

    for k in range(CHUNKS):
        first = 1 if k == 0 else 0
        blocks = ret_recv.at[pl.ds(k * chunk_blocks + first, chunk_blocks - first)]
        remote(blocks, blocks, ret_send_sem, ret_recv_sem.at[k], sibling).wait_recv()
        both = ret_recv[pl.ds(k * chunk_blocks, chunk_blocks)].astype(F32)
        out_rows = both[:, :cap].reshape(chunk_rows, width).astype(BF16)
        in_rows = both[:, cap:].reshape(chunk_rows, width).astype(BF16)
        cols = chunk_slice(k)
        sums = dot(comb_buf[0, :, cols], out_rows, 1, 0)
        sums = sums + dot(comb_buf[1, :, cols], out_rows, 1, 0)
        grads = dot(comb_buf[2, :, cols], in_rows, 1, 0)
        if k > 0:
            sums, grads = sums_buf[0] + sums, sums_buf[1] + grads
        if k < CHUNKS - 1:
            sums_buf[0] = sums
            sums_buf[1] = grads
        else:
            token_ref[0] = sums.T
            token_ref[1] = grads.T

    stores[0].start()

    blocks = send_buf.at[pl.ds(0, experts - 1)]
    remote(blocks, blocks, a2a_send_sem, a2a_recv_sem.at[0], sibling).wait_send()
    blocks = ret_send.at[pl.ds(1, experts - 1)]
    remote(blocks, blocks, ret_send_sem, ret_recv_sem.at[0], sibling).wait_send()
    for k in range(CHUNKS):
        pair_copy(k).wait_send()
        for n in range(far + near):
            rs_copy(k, n).wait_send()
            ag_copy(k, n).wait_send()
        for n in range(zs):
            sib_copy(k, 0, n).wait_send()
    for store in stores:
        store.wait()


def on_device(tokens, cotangent, w_in, w_out, route_token, route_count, copy_plan, route_prob):
    experts, cap = route_token.shape[1:]
    zs = lax.axis_size("dp") // 2
    nx = math.isqrt(experts)
    ny = experts // nx
    count, width = tokens.shape
    hidden = w_in.shape[2]
    half = hidden // 2
    slots = experts * cap
    chunk_rows = slots // CHUNKS
    own_rows = chunk_rows // zs
    hbm = pl.BlockSpec(memory_space=pltpu.HBM)
    dma = pltpu.SemaphoreType.DMA
    token_sums, weight_sums = pl.pallas_call(
        functools.partial(moe_kernel, experts, zs),
        out_shape=(
            jax.ShapeDtypeStruct((2, width, count), F32),
            jax.ShapeDtypeStruct((2, width, hidden), F32),
        ),
        in_specs=[hbm] * 9,
        out_specs=(hbm,) * 2,
        scratch_shapes=[
            pltpu.VMEM((width, count), BF16),
            pltpu.VMEM((width, count), BF16),
            pltpu.VMEM((width, hidden), BF16),
            pltpu.VMEM((width, hidden), BF16),
            pltpu.VMEM((cap, experts), jnp.int32),
            pltpu.VMEM((1, experts), jnp.int32),
            pltpu.VMEM((1, experts), jnp.int32),
            pltpu.VMEM((cap, experts), F32),
            pltpu.VMEM((2, experts), jnp.int32),
            pltpu.VMEM((experts, 2 * cap, width), BF16),
            pltpu.VMEM((experts, 2 * cap, width), BF16),
            pltpu.VMEM((slots, width), BF16),
            pltpu.VMEM((slots, width), BF16),
            pltpu.VMEM((CHUNKS, 2, chunk_rows, half), BF16),
            pltpu.VMEM((CHUNKS, 2, chunk_rows, half), BF16),
            pltpu.VMEM((CHUNKS, 2, chunk_rows, half), F32),
            pltpu.VMEM((CHUNKS, zs - 1, 2, own_rows, half), BF16),
            pltpu.VMEM((CHUNKS, zs - 1, 2, own_rows, half), BF16),
            pltpu.VMEM((2, 2, slots, half), BF16),
            pltpu.VMEM((experts, 2 * cap, width), BF16),
            pltpu.VMEM((experts, 2 * cap, width), BF16),
            pltpu.VMEM((3, count, slots), BF16),
            pltpu.VMEM((2, count, width), F32),
            pltpu.VMEM((2, width, count), F32),
            pltpu.VMEM((2, width, hidden), F32),
            dma((9,)),
            dma((2,)),
            dma,
            dma((CHUNKS,)),
            dma((CHUNKS,)),
            dma((CHUNKS,)),
            dma((CHUNKS, zs - 1)),
            dma((CHUNKS, zs - 1)),
            dma((CHUNKS, zs - 1)),
            dma((CHUNKS, zs - 1)),
            dma((CHUNKS, zs)),
            dma((CHUNKS,)),
            dma,
            dma((CHUNKS,)),
        ],
        compiler_params=pltpu.CompilerParams(
            collective_id=0, has_side_effects=True, vmem_limit_bytes=60 << 20
        ),
        name="moe_layer",
    )(
        tokens.T,
        cotangent.T,
        w_in[0],
        w_out[0].T,
        route_token[0].T,
        route_count,
        copy_plan[None],
        route_prob[0].T,
        jnp.asarray(offsets(ny, nx), jnp.int32).T,
    )
    out, tgrad = token_sums.astype(BF16)
    gin, gout = weight_sums.astype(BF16)
    return out.T, tgrad.T, gin[None], gout.T[None]


def solution(mesh):
    in_specs = (
        P("expert", "dp"),
        P("expert", "dp"),
        P("expert", "dp", None),
        P("expert", None, "dp"),
        P("expert", None, None),
        P("expert", None),
        P(),
        P("expert", None, None),
    )
    out_specs = (
        P("expert", "dp"),
        P("expert", "dp"),
        P("expert", "dp", None),
        P("expert", None, "dp"),
    )
    return jax.shard_map(
        on_device, mesh=mesh, in_specs=in_specs, out_specs=out_specs, check_vma=False
    )
```
